32 devices in a mesh: groups: 2 (over y), expert: 8 (over z, x), hidden: 2 (over core).
Axes of the slice: x: 2, y: 2, z: 4, core: 2. Of those that a mesh axis runs over, the one named last changes fastest.
Arguments:
- tokens: bfloat16 [128, 3072], P(('groups', 'expert'), 'hidden'), parts along dimension 0, may hold values from -6 to 6
- expert_ids: int32 [128, 4], P(('groups', 'expert')), parts along dimension 0, may hold values from 0 to 15, all different within a row; in each aligned block of 8 rows (0 to 7, 8 to 15, ...) at most 4 rows name the same one
- gate_codes: int32 [128, 4], P(('groups', 'expert')), parts along dimension 0, may hold values from 1 to 65535
- gate_weight: bfloat16 [8, 5376, 3072], P('expert', 'hidden'), may hold values from -0.109375 to 0.109375
- up_weight: bfloat16 [8, 5376, 3072], P('expert', 'hidden'), may hold values from -0.109375 to 0.109375
- down_weight: bfloat16 [8, 5376, 3072], P('expert', 'hidden'), may hold values from -0.078125 to 0.078125
Outputs:
- mixed: bfloat16 [128, 3072], P(('groups', 'expert'), 'hidden'), parts along dimension 0
The draws below stay inside these ranges and needn't reach their ends.
There are 2 independent parts, one for each index of `groups`. The reference program is written for one: setup_inputs(seed, part) draws one part's arguments, and reference() takes and returns one part's arrays. A program takes and returns all parts, laid end to end along the dimension named above; an argument that names none is the same for every part. Nothing has to cross between parts.
Inputs may be any that keep to these rules, and one draw needn't show every extreme that they name: `expert_ids`: each token names 4 different experts; experts numbered 8 or more are held elsewhere and add nothing here; the 8 tokens of one device name one expert at most 4 times, a bound that some block reaches.
All inputs are finite; a program needn't handle non-finite values.
Results may differ from the reference program's by a relative error of at most 0.009.
Values may be sent and summed in bfloat16 or wider, within the bound.
A program may use at most 128 MiB of HBM per device.

```python
import math
import jax
import jax.numpy as jnp
import numpy as np
from jax import lax

D = 3072
FF = 5376
ROUTED = 16
EXPERTS = 8
TOP = 4
TOK_DEV = 8
CAP = 4
TOKENS = 64
FF_S = 5376
FF_DEV = 2688
N_EXPERT = 8


def with_ends(drawn, rng, smallest, largest):
    extent = drawn.shape
    spot = [jax.random.randint(jax.random.fold_in(rng, axis), (), 0, extent[axis]) for axis in range(len(extent))]
    drawn = drawn.at[tuple(spot)].set(smallest)
    longest = extent.index(max(extent))
    spot[longest] = (spot[longest] + 1) % extent[longest]
    return drawn.at[tuple(spot)].set(largest)


def block_scale(stream_key, extent, shards, smallest, largest):
    gain, own = 1.0, jax.random.fold_in(stream_key, 6)
    for axis_at, blocks in shards:
        heights = jnp.exp(jax.random.uniform(jax.random.fold_in(own, axis_at), (blocks,), jnp.float32, smallest / len(shards), largest / len(shards)))
        gain = gain * jnp.repeat(heights, extent[axis_at] // blocks).reshape([-1 if axis == axis_at else 1 for axis in range(len(extent))])
    return gain


def assign_block(key, own, number, rows, amount, top, limit, skew):
    order = jax.random.permutation(key, amount)
    heavy_load, usual = portions_of(amount, rows * top, limit, skew, True), portions_of(amount, rows * top, limit, skew, False)
    places = jnp.arange(amount)

    def named(tallies, turn):
        used = int((tallies > 0).sum())
        fixed = max(1, used // 4)
        shifted = fixed + (places - fixed + turn * (used - fixed)) % max(1, amount - fixed)
        return jnp.zeros((amount,), jnp.int32).at[order[jnp.where(places < fixed, places, shifted)]].set(jnp.asarray(tallies, jnp.int32))

    tallies = jnp.where(number % 4 == 0, named(heavy_load, number // 4), named(usual, number - number // 4 - 1))
    mixed = jax.random.permutation(jax.random.fold_in(own, 3), amount)
    giver, taker = mixed[0:amount // 2 * 2:2], mixed[1:amount // 2 * 2:2]
    margin = jnp.minimum(tallies[giver] - 1, limit - tallies[taker]) // 2
    margin = jnp.where((giver == order[0]) | (taker == order[0]) | (tallies[taker] == 0), 0, jnp.maximum(margin, 0))
    shifted = jax.random.randint(jax.random.fold_in(own, 4), (amount // 2,), 0, 1 << 20) % (margin + 1)
    tallies = tallies.at[giver].add(-shifted).at[taker].add(shifted)
    labels = jnp.searchsorted(jnp.cumsum(tallies), jnp.arange(rows * top), side="right").astype(jnp.int32)
    table = labels.reshape(top, rows).T
    table = table[jax.random.permutation(jax.random.fold_in(own, 1), rows)]
    turn = jax.random.randint(jax.random.fold_in(own, 2), (rows, 1), 0, top)
    return jnp.take_along_axis(table, (jnp.arange(top)[None, :] + turn) % top, axis=1)


def portions_of(count, total, most, lean, full):
    portions = [(1 << 20) // math.isqrt(grade ** lean) + 1 for grade in range(1, count + 1)]
    largest = most if full else min(most, max(-(-total // count), total * portions[0] // sum(portions)))
    least = 1 if total - largest >= count - 1 else 0
    counts, surplus = [largest] + [least] * (count - 1), total - largest - least * (count - 1)
    while surplus > 0:
        free = [i for i in range(1, count) if counts[i] < largest] or [i for i in range(1, count) if counts[i] < most]
        mass, budget = sum([portions[i] for i in free]), surplus
        for i in free:
            addition = min(most - counts[i], max(1, budget * portions[i] // mass), surplus)
            counts[i] = counts[i] + addition
            surplus = surplus - addition
    return np.array(counts)


def gaussian(rng, extent, deviation, most, shards=(), kind=jnp.bfloat16):
    result = jax.random.normal(rng, extent, jnp.float32) * deviation
    if len(shards) > 0:
        result = block_scale(rng, extent, shards, -0.22, 0.18) * result
    return jnp.clip(result, min=-most, max=most).astype(kind)


def setup_inputs(seed: int = 0, part: int = 0) -> dict:
    keys = jax.random.split(jax.random.key(seed), 7)
    own_keys = jax.random.split(jax.random.fold_in(keys[6], part), 7)
    tokens = gaussian(own_keys[0], (TOKENS, D), 1.0, 6.0, ((0, 8), (1, 2)))
    expert_ids_keys = jax.random.split(jax.random.fold_in(own_keys[1], 1), TOKENS // TOK_DEV)
    expert_ids_turns = jax.random.permutation(jax.random.fold_in(own_keys[1], 3), TOKENS // TOK_DEV)
    expert_ids = jax.vmap(lambda own, number: assign_block(jax.random.fold_in(own_keys[1], 2), own, number, TOK_DEV, ROUTED, TOP, CAP, 2))(expert_ids_keys, expert_ids_turns).reshape((TOKENS, TOP))
    gate_codes = with_ends(jax.random.randint(own_keys[2], (TOKENS, TOP), 1, 65536), jax.random.fold_in(own_keys[2], 1), 1, 65535).astype(jnp.int32)
    gate_weight = gaussian(keys[3], (N_EXPERT, FF_S, D), D ** -0.5, 0.109375, ((0, 8), (1, 2)))
    up_weight = gaussian(keys[4], (N_EXPERT, FF_S, D), D ** -0.5, 0.109375, ((0, 8), (1, 2)))
    down_weight = gaussian(keys[5], (N_EXPERT, FF_S, D), FF ** -0.5, 0.078125, ((0, 8), (1, 2)))
    return dict(tokens=tokens, expert_ids=expert_ids, gate_codes=gate_codes, gate_weight=gate_weight, up_weight=up_weight, down_weight=down_weight)


def reference(tokens, expert_ids, gate_codes, gate_weight, up_weight, down_weight):
    blocks = TOKENS // TOK_DEV
    routes = TOK_DEV * TOP
    slices = N_EXPERT // EXPERTS
    pieces = FF // FF_DEV
    route_ids = expert_ids.reshape(blocks, routes)
    expert_range = jnp.arange(EXPERTS, dtype=jnp.int32)
    onehot = (route_ids[:, :, None] == expert_range[None, None, :]).astype(jnp.int32)
    position = jnp.sum((jnp.cumsum(onehot, axis=1) - onehot) * onehot, axis=2)
    token_of = (jnp.arange(blocks, dtype=jnp.int32)[:, None] * TOK_DEV
                + jnp.arange(routes, dtype=jnp.int32)[None, :] // TOP)
    gate_value = gate_codes.reshape(blocks, routes).astype(jnp.float32) / 32768.0
    slot_range = jnp.arange(CAP, dtype=jnp.int32)
    gate_split = gate_weight.reshape(slices, EXPERTS, FF_S, D)
    up_split = up_weight.reshape(slices, EXPERTS, FF_S, D)
    down_split = down_weight.reshape(slices, EXPERTS, FF_S, D)
    contract = (((1,), (1,)), ((), ()))

    def one_expert(expert, accumulated):
        slot_hit = (route_ids == expert)[:, :, None] & (position[:, :, None] == slot_range[None, None, :])
        hit_int = slot_hit.astype(jnp.int32)
        slot_token = jnp.sum(hit_int * token_of[:, :, None], axis=1).reshape(-1)
        slot_live = jnp.sum(hit_int, axis=1).reshape(-1).astype(jnp.float32)
        slot_gate = jnp.sum(slot_hit.astype(jnp.float32) * gate_value[:, :, None], axis=1).reshape(-1)
        slot_rows = jnp.take(tokens, slot_token, axis=0)
        w_gate = lax.dynamic_index_in_dim(gate_split, expert, 1, False).reshape(FF, D)
        w_up = lax.dynamic_index_in_dim(up_split, expert, 1, False).reshape(FF, D)
        w_down = lax.dynamic_index_in_dim(down_split, expert, 1, False).reshape(pieces, FF_DEV, D)
        gate_pre = lax.dot_general(slot_rows, w_gate, contract, preferred_element_type=jnp.float32)
        up_pre = lax.dot_general(slot_rows, w_up, contract, preferred_element_type=jnp.float32)
        hidden = (jax.nn.silu(gate_pre) * up_pre).astype(jnp.bfloat16)
        hidden_pieces = hidden.reshape(-1, pieces, FF_DEV)

        def add_piece(running, piece):
            piece_rows = lax.dynamic_index_in_dim(hidden_pieces, piece, 1, False)
            piece_down = lax.dynamic_index_in_dim(w_down, piece, 0, False)
            piece_out = jnp.dot(piece_rows, piece_down, preferred_element_type=jnp.float32)
            piece_out = lax.optimization_barrier(piece_out.astype(jnp.bfloat16)).astype(jnp.float32)
            return running + piece_out, None

        expert_out, _ = lax.scan(add_piece, jnp.zeros((blocks * CAP, D), jnp.float32),
                                 jnp.arange(pieces, dtype=jnp.int32))
        return accumulated.at[slot_token].add((slot_gate * slot_live)[:, None] * expert_out)

    accumulated = lax.fori_loop(0, EXPERTS, one_expert, jnp.zeros((TOKENS, D), jnp.float32))
    return accumulated.astype(jnp.bfloat16)
```

```python
import functools

import jax
import jax.numpy as jnp
from jax import lax
from jax.experimental import pallas as pl
from jax.experimental.pallas import tpu as pltpu
from jax.sharding import PartitionSpec as P

EXPERTS = 8
CAP = 4
GROUPS = 4
BLOCK = GROUPS * CAP
COLS = 512
STEP = 512
MESH = pl.DeviceIdType.MESH


def hidden_steps(units):
    return [(at, min(STEP, units - at)) for at in range(0, units, STEP)]


def iota(shape, axis):
    return lax.broadcasted_iota(jnp.int32, shape, axis)


def moe_kernel(
    n, tok_ref, ids_ref, codes_ref, gate_hbm, up_hbm, down_hbm, out_ref,
    w_gate, w_up, w_down, send_rows, got_rows, rows, hidden, send_out, got_out,
    gate_sem, up_sem, down_sem, rows_sent, rows_got, out_sent, out_got,
):
    tok_dev, half = tok_ref.shape
    units, width = gate_hbm.shape[1:]
    steps = hidden_steps(units)
    per_half = half // COLS
    order = [part * per_half + at for at in range(per_half) for part in range(2)]
    group = lax.axis_index("groups")
    me = lax.axis_index("expert")
    core = lax.axis_index("hidden")

    gate_copy = [
        pltpu.make_async_copy(
            gate_hbm.at[0, pl.ds(at, size)], w_gate.at[pl.ds(at, size)], gate_sem.at[j]
        )
        for j, (at, size) in enumerate(steps)
    ]
    up_copy = [
        pltpu.make_async_copy(
            up_hbm.at[0, pl.ds(at, size)], w_up.at[pl.ds(at, size)], up_sem.at[j]
        )
        for j, (at, size) in enumerate(steps)
    ]
    down_copy = {
        c: pltpu.make_async_copy(
            down_hbm.at[0, :, pl.ds(c * COLS, COLS)], w_down.at[c], down_sem.at[c]
        )
        for c in order
    }
    for j in range(len(steps)):
        gate_copy[j].start()
        up_copy[j].start()
    for c in order:
        down_copy[c].start()

    barrier = pltpu.get_barrier_semaphore()

    @pl.loop(1, n)
    def _(k):
        other = lax.rem(me + k, n)
        for part in range(2):
            pl.semaphore_signal(
                barrier, inc=1, device_id=(group, other, part), device_id_type=MESH
            )

    pl.semaphore_signal(barrier, inc=1, device_id=(group, me, 1 - core), device_id_type=MESH)

    stacked = GROUPS * tok_dev
    slots = (stacked, EXPERTS * BLOCK)
    row, col = iota(slots, 0), iota(slots, 1)
    ids = jnp.concatenate([ids_ref[...]] * GROUPS, axis=0)
    codes = jnp.concatenate([codes_ref[...]] * GROUPS, axis=0)
    named = jnp.zeros(slots, jnp.bool_)
    code = jnp.zeros(slots, jnp.int32)
    for k in range(ids.shape[1]):
        same = ids[:, k:k + 1] == col // BLOCK
        named = named | same
        code = code + jnp.where(same, codes[:, k:k + 1], 0)
    square = (stacked, stacked)
    a, b = iota(square, 0), iota(square, 1)
    earlier = (a // tok_dev == b // tok_dev) & (b < a)
    place = jnp.dot(
        earlier.astype(jnp.float32).astype(jnp.bfloat16),
        named.astype(jnp.float32).astype(jnp.bfloat16),
        preferred_element_type=jnp.float32,
    ).astype(jnp.int32)
    hit = named & (place == col % CAP) & ((col // CAP) % GROUPS == row // tok_dev)
    pick = hit.astype(jnp.float32)
    high = pick * (code // 256).astype(jnp.float32) / 128.0
    low = pick * (code % 256).astype(jnp.float32) / 32768.0
    gains = jnp.concatenate([high, low], axis=0).astype(jnp.bfloat16)

    tok = tok_ref[...].astype(jnp.float32)
    piece = half // GROUPS
    tall = jnp.concatenate(
        [tok[:, g * piece:(g + 1) * piece] for g in range(GROUPS)], axis=0
    ).astype(jnp.bfloat16)
    send_rows[...] = (
        lax.dot_general(
            pick.T.astype(jnp.bfloat16), tall, (((1,), (0,)), ((), ())),
            preferred_element_type=jnp.float32,
        )
        .astype(jnp.bfloat16)
        .reshape(EXPERTS, BLOCK, piece)
    )

    pl.semaphore_wait(barrier, 2 * n - 1)

    def rows_to(other, part):
        return pltpu.make_async_remote_copy(
            src_ref=send_rows.at[lax.rem(other, EXPERTS)],
            dst_ref=got_rows.at[core * n + me],
            send_sem=rows_sent,
            recv_sem=rows_got,
            device_id=(group, other, part),
            device_id_type=MESH,
        )

    @pl.loop(1, n)
    def _(k):
        other = lax.rem(me + k, n)
        for part in range(2):
            rows_to(other, part).start()

    rows_to(me, 1 - core).start()
    pltpu.make_async_copy(
        send_rows.at[lax.rem(me, EXPERTS)], got_rows.at[core * n + me], rows_got
    ).start()

    flat = EXPERTS * BLOCK
    lot = EXPERTS * CAP
    a, b = iota((flat, flat), 0), iota((flat, flat), 1)
    split = (a // lot) == (b // CAP) % GROUPS
    split = split & ((a % lot) // CAP == b // BLOCK) & (a % CAP == b % CAP)
    split = split.astype(jnp.float32).astype(jnp.bfloat16)
    join = (b // lot) == (a // CAP) % GROUPS
    join = join & ((b % lot) // CAP == a // BLOCK) & (b % CAP == a % CAP)
    join = join.astype(jnp.float32).astype(jnp.bfloat16)

    pltpu.make_async_copy(got_rows, got_rows, rows_got).wait()
    for s in range(n // EXPERTS):
        for part in range(2):
            block = got_rows[part * n + s * EXPERTS:part * n + (s + 1) * EXPERTS]
            block = jnp.dot(
                split, block.reshape(flat, piece), preferred_element_type=jnp.float32
            ).astype(jnp.bfloat16)
            for g in range(GROUPS):
                at = part * half + g * piece
                rows[s * lot:(s + 1) * lot, at:at + piece] = block[g * lot:(g + 1) * lot]

    contract = (((1,), (1,)), ((), ()))
    for j, (at, size) in enumerate(steps):
        gate_copy[j].wait()
        gate_pre = lax.dot_general(
            rows[...], w_gate[at:at + size], contract, preferred_element_type=jnp.float32
        )
        up_copy[j].wait()
        up_pre = lax.dot_general(
            rows[...], w_up[at:at + size], contract, preferred_element_type=jnp.float32
        )
        silu = gate_pre / (1.0 + jnp.exp(-gate_pre))
        hidden[:, at:at + size] = (silu * up_pre).astype(jnp.bfloat16)

    lane = COLS // GROUPS
    for c in order:
        part, at = c // per_half, c % per_half
        down_copy[c].wait()
        out = jnp.dot(hidden[...], w_down[c], preferred_element_type=jnp.float32)
        out = out.astype(jnp.bfloat16)
        for s in range(n // EXPERTS):
            block = jnp.concatenate(
                [
                    out[s * lot:(s + 1) * lot, g * lane:(g + 1) * lane]
                    for g in range(GROUPS)
                ],
                axis=0,
            )
            send_out[c, s * EXPERTS:(s + 1) * EXPERTS] = (
                jnp.dot(join, block, preferred_element_type=jnp.float32)
                .astype(jnp.bfloat16)
                .reshape(EXPERTS, BLOCK, lane)
            )

        def out_to(other):
            return pltpu.make_async_remote_copy(
                src_ref=send_out.at[c, other],
                dst_ref=got_out.at[(at * 2 + core) * n + me],
                send_sem=out_sent,
                recv_sem=out_got.at[at],
                device_id=(group, other, part),
                device_id_type=MESH,
            )

        @pl.loop(1, n)
        def _(k):
            out_to(lax.rem(me + k, n)).start()

        @pl.when(core == part)
        def _():
            pltpu.make_async_copy(
                send_out.at[c, me], got_out.at[(at * 2 + core) * n + me], out_got.at[at]
            ).start()

        @pl.when(core != part)
        def _():
            out_to(me).start()

    for at in range(per_half):
        landed = got_out.at[pl.ds(at * 2 * n, 2 * n)]
        pltpu.make_async_copy(landed, landed, out_got.at[at]).wait()
        total = jnp.zeros((2 * stacked, lane), jnp.float32)
        for s in range(2 * n // EXPERTS):
            first = at * 2 * n + s * EXPERTS
            block = got_out[first:first + EXPERTS].reshape(flat, lane)
            total = total + jnp.dot(gains, block, preferred_element_type=jnp.float32)
        mixed = total[:stacked] + total[stacked:]
        for g in range(GROUPS):
            to = at * COLS + g * lane
            out_ref[:, to:to + lane] = mixed[g * tok_dev:(g + 1) * tok_dev].astype(
                out_ref.dtype
            )

    sent = got_rows.at[pl.ds(0, 2 * n - 1)]
    pltpu.make_async_copy(sent, sent, rows_sent).wait()
    sent = got_out.at[pl.ds(0, 2 * per_half * n - per_half)]
    pltpu.make_async_copy(sent, sent, out_sent).wait()


def per_device(tokens, expert_ids, gate_codes, gate_weight, up_weight, down_weight):
    n = lax.axis_size("expert")
    tok_dev, half = tokens.shape
    units, width = gate_weight.shape[1:]
    parts = len(hidden_steps(units))
    columns = width // COLS
    piece = half // GROUPS
    bf16 = jnp.bfloat16
    return pl.pallas_call(
        functools.partial(moe_kernel, n),
        out_shape=jax.ShapeDtypeStruct((tok_dev, half), bf16),
        in_specs=[pl.BlockSpec(memory_space=pltpu.VMEM)] * 3
        + [pl.BlockSpec(memory_space=pl.ANY)] * 3,
        out_specs=pl.BlockSpec(memory_space=pltpu.VMEM),
        scratch_shapes=[
            pltpu.VMEM((units, width), bf16),
            pltpu.VMEM((units, width), bf16),
            pltpu.VMEM((columns, units, COLS), bf16),
            pltpu.VMEM((EXPERTS, BLOCK, piece), bf16),
            pltpu.VMEM((2 * n, BLOCK, piece), bf16),
            pltpu.VMEM((n * CAP, width), bf16),
            pltpu.VMEM((n * CAP, units), bf16),
            pltpu.VMEM((columns, n, BLOCK, COLS // GROUPS), bf16),
            pltpu.VMEM((columns * n, BLOCK, COLS // GROUPS), bf16),
            pltpu.SemaphoreType.DMA((parts,)),
            pltpu.SemaphoreType.DMA((parts,)),
            pltpu.SemaphoreType.DMA((columns,)),
            pltpu.SemaphoreType.DMA,
            pltpu.SemaphoreType.DMA,
            pltpu.SemaphoreType.DMA,
            pltpu.SemaphoreType.DMA((half // COLS,)),
        ],
        compiler_params=pltpu.CompilerParams(
            collective_id=0, has_side_effects=True, vmem_limit_bytes=58 * 1024 * 1024
        ),
    )(tokens, expert_ids, gate_codes, gate_weight, up_weight, down_weight)


def solution(mesh):
    in_specs = (
        P(("groups", "expert"), "hidden"),
        P(("groups", "expert"), None),
        P(("groups", "expert"), None),
        P("expert", "hidden", None),
        P("expert", "hidden", None),
        P("expert", "hidden", None),
    )
    out_specs = P(("groups", "expert"), "hidden")
    return jax.shard_map(
        per_device, mesh=mesh, in_specs=in_specs, out_specs=out_specs, check_vma=False
    )
```

```python
import functools

import jax
import jax.numpy as jnp
from jax import lax
from jax.experimental import pallas as pl
from jax.experimental.pallas import tpu as pltpu
from jax.sharding import PartitionSpec as P

EXPERTS = 8
CAP = 4
GROUPS = 4
BLOCK = GROUPS * CAP
COLS = 512
STEP = 512
MESH = pl.DeviceIdType.MESH


def hidden_steps(units):
    return [(at, min(STEP, units - at)) for at in range(0, units, STEP)]


def iota(shape, axis):
    return lax.broadcasted_iota(jnp.int32, shape, axis)


def moe_kernel(
    n, tok_ref, ids_ref, codes_ref, gate_hbm, up_hbm, down_hbm, out_ref,
    w_gate, w_up, w_down, send_rows, got_rows, rows, hidden, send_out, pair_out,
    got_out, gate_sem, up_sem, down_sem, rows_sent, rows_got, share_sem, pair_sem, out_sent,
    out_got,
):
    tok_dev, half = tok_ref.shape
    units, width = gate_hbm.shape[1:]
    steps = hidden_steps(units)
    per_half = half // COLS
    group = lax.axis_index("groups")
    me = lax.axis_index("expert")
    core = lax.axis_index("hidden")

    column = [pl.multiple_of(core * half, half), pl.multiple_of((1 - core) * half, half)]

    def fetch(source, target, sems, j, side):
        at, size = steps[j]
        return pltpu.make_async_copy(
            source.at[0, pl.ds(at, size), pl.ds(column[side], half)],
            target.at[side, pl.ds(at, size)],
            sems.at[side, j],
        )

    gate_copy = [[fetch(gate_hbm, w_gate, gate_sem, j, i) for i in range(2)] for j in range(len(steps))]
    up_copy = [[fetch(up_hbm, w_up, up_sem, j, i) for i in range(2)] for j in range(len(steps))]
    down_copy = [
        pltpu.make_async_copy(
            down_hbm.at[
                0, :, pl.ds(pl.multiple_of(column[1 - c // per_half] + c % per_half * COLS, COLS), COLS)
            ],
            w_down.at[c],
            down_sem.at[c],
        )
        for c in range(2 * per_half)
    ]
    for j in range(len(steps)):
        for side in range(2):
            gate_copy[j][side].start()
            up_copy[j][side].start()
    for copy in down_copy:
        copy.start()

    barrier = pltpu.get_barrier_semaphore()

    @pl.loop(1, n)
    def _(k):
        other = lax.rem(me + k, n)
        pl.semaphore_signal(barrier, inc=1, device_id=(group, other, core), device_id_type=MESH)

    pl.semaphore_signal(barrier, inc=1, device_id=(group, me, 1 - core), device_id_type=MESH)

    stacked = GROUPS * tok_dev
    slots = (stacked, EXPERTS * BLOCK)
    row, col = iota(slots, 0), iota(slots, 1)
    ids = jnp.concatenate([ids_ref[...].T] * GROUPS, axis=0)
    codes = jnp.concatenate([codes_ref[...].T] * GROUPS, axis=0)
    named = jnp.zeros(slots, jnp.bool_)
    code = jnp.zeros(slots, jnp.int32)
    for k in range(ids.shape[1]):
        same = ids[:, k:k + 1] == col // BLOCK
        named = named | same
        code = code + jnp.where(same, codes[:, k:k + 1], 0)
    square = (stacked, stacked)
    a, b = iota(square, 0), iota(square, 1)
    earlier = (a // tok_dev == b // tok_dev) & (b < a)
    place = jnp.dot(
        earlier.astype(jnp.float32).astype(jnp.bfloat16),
        named.astype(jnp.float32).astype(jnp.bfloat16),
        preferred_element_type=jnp.float32,
    ).astype(jnp.int32)
    hit = named & (place == col % CAP) & ((col // CAP) % GROUPS == row // tok_dev)
    pick = hit.astype(jnp.float32)
    high = pick * (code // 256).astype(jnp.float32) / 128.0
    low = pick * (code % 256).astype(jnp.float32) / 32768.0
    gains = jnp.concatenate([high, low], axis=0).astype(jnp.bfloat16)

    tok = tok_ref[...].astype(jnp.float32)
    piece = half // GROUPS
    tall = jnp.concatenate(
        [tok[:, g * piece:(g + 1) * piece] for g in range(GROUPS)], axis=0
    ).astype(jnp.bfloat16)
    send_rows[...] = (
        lax.dot_general(
            pick.T.astype(jnp.bfloat16), tall, (((1,), (0,)), ((), ())),
            preferred_element_type=jnp.float32,
        )
        .astype(jnp.bfloat16)
        .reshape(EXPERTS, BLOCK, piece)
    )

    pl.semaphore_wait(barrier, n)

    @pl.loop(1, n)
    def _(k):
        other = lax.rem(me + k, n)
        pltpu.make_async_remote_copy(
            src_ref=send_rows.at[lax.rem(other, EXPERTS)],
            dst_ref=got_rows.at[0, me],
            send_sem=rows_sent,
            recv_sem=rows_got,
            device_id=(group, other, core),
            device_id_type=MESH,
        ).start()

    pltpu.make_async_copy(
        send_rows.at[lax.rem(me, EXPERTS)], got_rows.at[0, me], rows_got
    ).start()

    flat = EXPERTS * BLOCK
    lot = EXPERTS * CAP
    a, b = iota((flat, flat), 0), iota((flat, flat), 1)
    split = (a // lot) == (b // CAP) % GROUPS
    split = split & ((a % lot) // CAP == b // BLOCK) & (a % CAP == b % CAP)
    split = split.astype(jnp.float32).astype(jnp.bfloat16)
    join = (b // lot) == (a // CAP) % GROUPS
    join = join & ((b % lot) // CAP == a // BLOCK) & (b % CAP == a % CAP)
    join = join.astype(jnp.float32).astype(jnp.bfloat16)

    pltpu.make_async_copy(got_rows.at[0], got_rows.at[0], rows_got).wait()
    share = pltpu.make_async_remote_copy(
        src_ref=got_rows.at[0],
        dst_ref=got_rows.at[1],
        send_sem=share_sem.at[0],
        recv_sem=share_sem.at[1],
        device_id=(group, me, 1 - core),
        device_id_type=MESH,
    )
    share.start()

    def place_rows(side):
        for s in range(n // EXPERTS):
            block = got_rows[side, s * EXPERTS:(s + 1) * EXPERTS]
            block = jnp.dot(
                split, block.reshape(flat, piece), preferred_element_type=jnp.float32
            ).astype(jnp.bfloat16)
            for g in range(GROUPS):
                rows[side, s * lot:(s + 1) * lot, g * piece:(g + 1) * piece] = block[
                    g * lot:(g + 1) * lot
                ]

    def project(copies, weight, j, side):
        at, size = steps[j]
        copies[j][side].wait()
        return lax.dot_general(
            rows[side], weight[side, at:at + size], (((1,), (1,)), ((), ())),
            preferred_element_type=jnp.float32,
        )

    place_rows(0)
    for j, (at, size) in enumerate(steps):
        gate_pre = project(gate_copy, w_gate, j, 0)
        up_pre = project(up_copy, w_up, j, 0)
        if j == 0:
            share.wait()
            place_rows(1)
        gate_pre = gate_pre + project(gate_copy, w_gate, j, 1)
        up_pre = up_pre + project(up_copy, w_up, j, 1)
        silu = gate_pre / (1.0 + jnp.exp(-gate_pre))
        hidden[:, at:at + size] = (silu * up_pre).astype(jnp.bfloat16)

    lane = COLS // GROUPS
    pair = [
        pltpu.make_async_remote_copy(
            src_ref=send_out.at[c],
            dst_ref=pair_out.at[c],
            send_sem=pair_sem.at[0, c],
            recv_sem=pair_sem.at[1, c],
            device_id=(group, me, 1 - core),
            device_id_type=MESH,
        )
        for c in range(per_half)
    ]
    for c in range(2 * per_half):
        at = c % per_half
        down_copy[c].wait()
        out = jnp.dot(hidden[...], w_down[c], preferred_element_type=jnp.float32)
        out = out.astype(jnp.bfloat16)
        if c >= per_half:
            pair[at].wait_recv()
        for s in range(n // EXPERTS):
            span = slice(s * EXPERTS, (s + 1) * EXPERTS)
            block = jnp.concatenate(
                [
                    out[s * lot:(s + 1) * lot, g * lane:(g + 1) * lane]
                    for g in range(GROUPS)
                ],
                axis=0,
            )
            block = jnp.dot(join, block, preferred_element_type=jnp.float32)
            if c >= per_half:
                block = block + pair_out[at, span].reshape(flat, lane).astype(jnp.float32)
            send_out[c, span] = block.astype(jnp.bfloat16).reshape(EXPERTS, BLOCK, lane)
        if c < per_half:
            pair[c].start()
        else:

            @pl.loop(1, n)
            def _(k):
                other = lax.rem(me + k, n)
                pltpu.make_async_remote_copy(
                    src_ref=send_out.at[c, other],
                    dst_ref=got_out.at[at, me],
                    send_sem=out_sent.at[at],
                    recv_sem=out_got.at[at],
                    device_id=(group, other, core),
                    device_id_type=MESH,
                ).start()

            pltpu.make_async_copy(
                send_out.at[c, me], got_out.at[at, me], out_got.at[at]
            ).start()

    for at in range(per_half):
        landed = got_out.at[at]
        pltpu.make_async_copy(landed, landed, out_got.at[at]).wait()
        total = jnp.zeros((2 * stacked, lane), jnp.float32)
        for s in range(n // EXPERTS):
            block = got_out[at, s * EXPERTS:(s + 1) * EXPERTS].reshape(flat, lane)
            total = total + jnp.dot(gains, block, preferred_element_type=jnp.float32)
        mixed = total[:stacked] + total[stacked:]
        for g in range(GROUPS):
            to = at * COLS + g * lane
            out_ref[:, to:to + lane] = mixed[g * tok_dev:(g + 1) * tok_dev].astype(
                out_ref.dtype
            )

    for copy in pair:
        copy.wait_send()
    sent = got_rows.at[0, pl.ds(0, n - 1)]
    pltpu.make_async_copy(sent, sent, rows_sent).wait()
    for at in range(per_half):
        sent = got_out.at[at, pl.ds(0, n - 1)]
        pltpu.make_async_copy(sent, sent, out_sent.at[at]).wait()


def per_device(tokens, expert_ids, gate_codes, gate_weight, up_weight, down_weight):
    n = lax.axis_size("expert")
    tok_dev, half = tokens.shape
    units, width = gate_weight.shape[1:]
    parts = len(hidden_steps(units))
    columns = width // COLS
    lane = COLS // GROUPS
    piece = half // GROUPS
    bf16 = jnp.bfloat16
    return pl.pallas_call(
        functools.partial(moe_kernel, n),
        out_shape=jax.ShapeDtypeStruct((tok_dev, half), bf16),
        in_specs=[pl.BlockSpec(memory_space=pltpu.VMEM)] * 3
        + [pl.BlockSpec(memory_space=pl.ANY)] * 3,
        out_specs=pl.BlockSpec(memory_space=pltpu.VMEM),
        scratch_shapes=[
            pltpu.VMEM((2, units, half), bf16),
            pltpu.VMEM((2, units, half), bf16),
            pltpu.VMEM((columns, units, COLS), bf16),
            pltpu.VMEM((EXPERTS, BLOCK, piece), bf16),
            pltpu.VMEM((2, n, BLOCK, piece), bf16),
            pltpu.VMEM((2, n * CAP, half), bf16),
            pltpu.VMEM((n * CAP, units), bf16),
            pltpu.VMEM((columns, n, BLOCK, lane), bf16),
            pltpu.VMEM((half // COLS, n, BLOCK, lane), bf16),
            pltpu.VMEM((half // COLS, n, BLOCK, lane), bf16),
            pltpu.SemaphoreType.DMA((2, parts)),
            pltpu.SemaphoreType.DMA((2, parts)),
            pltpu.SemaphoreType.DMA((columns,)),
            pltpu.SemaphoreType.DMA,
            pltpu.SemaphoreType.DMA,
            pltpu.SemaphoreType.DMA((2,)),
            pltpu.SemaphoreType.DMA((2, half // COLS)),
            pltpu.SemaphoreType.DMA((half // COLS,)),
            pltpu.SemaphoreType.DMA((half // COLS,)),
        ],
        compiler_params=pltpu.CompilerParams(
            collective_id=0, has_side_effects=True, vmem_limit_bytes=58 * 1024 * 1024
        ),
    )(tokens, expert_ids.T, gate_codes.T, gate_weight, up_weight, down_weight)


def solution(mesh):
    in_specs = (
        P(("groups", "expert"), "hidden"),
        P(("groups", "expert"), None),
        P(("groups", "expert"), None),
        P("expert", "hidden", None),
        P("expert", "hidden", None),
        P("expert", "hidden", None),
    )
    out_specs = P(("groups", "expert"), "hidden")
    return jax.shard_map(
        per_device, mesh=mesh, in_specs=in_specs, out_specs=out_specs, check_vma=False
    )
```

```python
import functools

import jax
import jax.numpy as jnp
from jax import lax
from jax.experimental import pallas as pl
from jax.experimental.pallas import tpu as pltpu
from jax.sharding import PartitionSpec as P

EXPERTS = 8
CAP = 4
GROUPS = 4
BLOCK = GROUPS * CAP
COLS = 512
STEP = 896
MESH = pl.DeviceIdType.MESH


def hidden_steps(units):
    return [(at, min(STEP, units - at)) for at in range(0, units, STEP)]


def iota(shape, axis):
    return lax.broadcasted_iota(jnp.int32, shape, axis)


def moe_kernel(
    n, tok_ref, ids_ref, codes_ref, gate_hbm, up_hbm, down_hbm, out_ref,
    w_gate, w_up, w_down, send_rows, got_rows, rows, hidden, send_out, pair_out,
    got_out, gate_sem, up_sem, down_sem, rows_sent, rows_got, share_sem, pair_sem, out_sent,
    out_got,
):
    tok_dev, half = tok_ref.shape
    units, width = gate_hbm.shape[1:]
    steps = hidden_steps(units)
    per_half = half // COLS
    group = lax.axis_index("groups")
    me = lax.axis_index("expert")
    core = lax.axis_index("hidden")

    barrier = pltpu.get_barrier_semaphore()

    @pl.loop(1, n)
    def _(k):
        other = lax.rem(me + k, n)
        pl.semaphore_signal(barrier, inc=1, device_id=(group, other, core), device_id_type=MESH)

    pl.semaphore_signal(barrier, inc=1, device_id=(group, me, 1 - core), device_id_type=MESH)

    column = [pl.multiple_of(core * half, half), pl.multiple_of((1 - core) * half, half)]

    def fetch(source, target, sems, j, side):
        at, size = steps[j]
        return pltpu.make_async_copy(
            source.at[0, pl.ds(at, size), pl.ds(column[side], half)],
            target.at[side, pl.ds(at, size)],
            sems.at[side, j],
        )

    gate_copy = [[fetch(gate_hbm, w_gate, gate_sem, j, i) for i in range(2)] for j in range(len(steps))]
    up_copy = [[fetch(up_hbm, w_up, up_sem, j, i) for i in range(2)] for j in range(len(steps))]
    down_copy = [
        pltpu.make_async_copy(
            down_hbm.at[
                0, :, pl.ds(pl.multiple_of(column[1 - c // per_half] + c % per_half * COLS, COLS), COLS)
            ],
            w_down.at[c],
            down_sem.at[c],
        )
        for c in range(2 * per_half)
    ]
    def start_weights(some):
        for j in some:
            for side in range(2):
                gate_copy[j][side].start()
                up_copy[j][side].start()

    early = min(2, len(steps))
    start_weights(range(early))

    stacked = GROUPS * tok_dev
    slots = (stacked, EXPERTS * BLOCK)
    row, col = iota(slots, 0), iota(slots, 1)
    ids = jnp.concatenate([ids_ref[...].T] * GROUPS, axis=0)
    codes = jnp.concatenate([codes_ref[...].T] * GROUPS, axis=0)
    named = jnp.zeros(slots, jnp.bool_)
    code = jnp.zeros(slots, jnp.int32)
    for k in range(ids.shape[1]):
        same = ids[:, k:k + 1] == col // BLOCK
        named = named | same
        code = code + jnp.where(same, codes[:, k:k + 1], 0)
    square = (stacked, stacked)
    a, b = iota(square, 0), iota(square, 1)
    earlier = (a // tok_dev == b // tok_dev) & (b < a)
    place = jnp.dot(
        earlier.astype(jnp.float32).astype(jnp.bfloat16),
        named.astype(jnp.float32).astype(jnp.bfloat16),
        preferred_element_type=jnp.float32,
    ).astype(jnp.int32)
    hit = named & (place == col % CAP) & ((col // CAP) % GROUPS == row // tok_dev)
    pick = hit.astype(jnp.float32)
    high = pick * (code // 256).astype(jnp.float32) / 128.0
    low = pick * (code % 256).astype(jnp.float32) / 32768.0
    gains = jnp.concatenate([high, low], axis=0).astype(jnp.bfloat16)

    tok = tok_ref[...].astype(jnp.float32)
    piece = half // GROUPS
    tall = jnp.concatenate(
        [tok[:, g * piece:(g + 1) * piece] for g in range(GROUPS)], axis=0
    ).astype(jnp.bfloat16)
    send_rows[...] = (
        lax.dot_general(
            pick.T.astype(jnp.bfloat16), tall, (((1,), (0,)), ((), ())),
            preferred_element_type=jnp.float32,
        )
        .astype(jnp.bfloat16)
        .reshape(EXPERTS, BLOCK, piece)
    )

    pl.semaphore_wait(barrier, n)

    @pl.loop(1, n)
    def _(k):
        other = lax.rem(me + k, n)
        pltpu.make_async_remote_copy(
            src_ref=send_rows.at[lax.rem(other, EXPERTS)],
            dst_ref=got_rows.at[0, me],
            send_sem=rows_sent,
            recv_sem=rows_got,
            device_id=(group, other, core),
            device_id_type=MESH,
        ).start()

    pltpu.make_async_copy(
        send_rows.at[lax.rem(me, EXPERTS)], got_rows.at[0, me], rows_got
    ).start()

    start_weights(range(early, len(steps)))
    for copy in down_copy:
        copy.start()

    flat = EXPERTS * BLOCK
    lot = EXPERTS * CAP
    a, b = iota((flat, flat), 0), iota((flat, flat), 1)
    split = (a // lot) == (b // CAP) % GROUPS
    split = split & ((a % lot) // CAP == b // BLOCK) & (a % CAP == b % CAP)
    split = split.astype(jnp.float32).astype(jnp.bfloat16)
    join = (b // lot) == (a // CAP) % GROUPS
    join = join & ((b % lot) // CAP == a // BLOCK) & (b % CAP == a % CAP)
    join = join.astype(jnp.float32).astype(jnp.bfloat16)

    pltpu.make_async_copy(got_rows.at[0], got_rows.at[0], rows_got).wait()
    share = pltpu.make_async_remote_copy(
        src_ref=got_rows.at[0],
        dst_ref=got_rows.at[1],
        send_sem=share_sem.at[0],
        recv_sem=share_sem.at[1],
        device_id=(group, me, 1 - core),
        device_id_type=MESH,
    )
    share.start()

    def place_rows(side):
        for s in range(n // EXPERTS):
            block = got_rows[side, s * EXPERTS:(s + 1) * EXPERTS]
            block = jnp.dot(
                split, block.reshape(flat, piece), preferred_element_type=jnp.float32
            ).astype(jnp.bfloat16)
            for g in range(GROUPS):
                rows[side, s * lot:(s + 1) * lot, g * piece:(g + 1) * piece] = block[
                    g * lot:(g + 1) * lot
                ]

    def project(copies, weight, j, side):
        at, size = steps[j]
        copies[j][side].wait()
        return lax.dot_general(
            rows[side], weight[side, at:at + size], (((1,), (1,)), ((), ())),
            preferred_element_type=jnp.float32,
        )

    place_rows(0)
    for j, (at, size) in enumerate(steps):
        gate_pre = project(gate_copy, w_gate, j, 0)
        up_pre = project(up_copy, w_up, j, 0)
        if j == 0:
            share.wait()
            place_rows(1)
        gate_pre = gate_pre + project(gate_copy, w_gate, j, 1)
        up_pre = up_pre + project(up_copy, w_up, j, 1)
        silu = gate_pre / (1.0 + jnp.exp(-gate_pre))
        hidden[:, at:at + size] = (silu * up_pre).astype(jnp.bfloat16)

    lane = COLS // GROUPS
    pair = [
        pltpu.make_async_remote_copy(
            src_ref=send_out.at[c],
            dst_ref=pair_out.at[c],
            send_sem=pair_sem.at[0, c],
            recv_sem=pair_sem.at[1, c],
            device_id=(group, me, 1 - core),
            device_id_type=MESH,
        )
        for c in range(per_half)
    ]
    for c in range(2 * per_half):
        at = c % per_half
        down_copy[c].wait()
        out = jnp.dot(hidden[...], w_down[c], preferred_element_type=jnp.float32)
        out = out.astype(jnp.bfloat16)
        if c >= per_half:
            pair[at].wait_recv()
        for s in range(n // EXPERTS):
            span = slice(s * EXPERTS, (s + 1) * EXPERTS)
            block = jnp.concatenate(
                [
                    out[s * lot:(s + 1) * lot, g * lane:(g + 1) * lane]
                    for g in range(GROUPS)
                ],
                axis=0,
            )
            block = jnp.dot(join, block, preferred_element_type=jnp.float32)
            if c >= per_half:
                block = block + pair_out[at, span].reshape(flat, lane).astype(jnp.float32)
            send_out[c, span] = block.astype(jnp.bfloat16).reshape(EXPERTS, BLOCK, lane)
        if c < per_half:
            pair[c].start()
        else:

            @pl.loop(1, n)
            def _(k):
                other = lax.rem(me + k, n)
                pltpu.make_async_remote_copy(
                    src_ref=send_out.at[c, other],
                    dst_ref=got_out.at[at, me],
                    send_sem=out_sent.at[at],
                    recv_sem=out_got.at[at],
                    device_id=(group, other, core),
                    device_id_type=MESH,
                ).start()

            pltpu.make_async_copy(
                send_out.at[c, me], got_out.at[at, me], out_got.at[at]
            ).start()

    for at in range(per_half):
        landed = got_out.at[at]
        pltpu.make_async_copy(landed, landed, out_got.at[at]).wait()
        total = jnp.zeros((2 * stacked, lane), jnp.float32)
        for s in range(n // EXPERTS):
            block = got_out[at, s * EXPERTS:(s + 1) * EXPERTS].reshape(flat, lane)
            total = total + jnp.dot(gains, block, preferred_element_type=jnp.float32)
        mixed = total[:stacked] + total[stacked:]
        for g in range(GROUPS):
            to = at * COLS + g * lane
            out_ref[:, to:to + lane] = mixed[g * tok_dev:(g + 1) * tok_dev].astype(
                out_ref.dtype
            )

    for copy in pair:
        copy.wait_send()
    sent = got_rows.at[0, pl.ds(0, n - 1)]
    pltpu.make_async_copy(sent, sent, rows_sent).wait()
    for at in range(per_half):
        sent = got_out.at[at, pl.ds(0, n - 1)]
        pltpu.make_async_copy(sent, sent, out_sent.at[at]).wait()


def per_device(tokens, expert_ids, gate_codes, gate_weight, up_weight, down_weight):
    n = lax.axis_size("expert")
    tok_dev, half = tokens.shape
    units, width = gate_weight.shape[1:]
    parts = len(hidden_steps(units))
    columns = width // COLS
    lane = COLS // GROUPS
    piece = half // GROUPS
    bf16 = jnp.bfloat16
    return pl.pallas_call(
        functools.partial(moe_kernel, n),
        out_shape=jax.ShapeDtypeStruct((tok_dev, half), bf16),
        in_specs=[pl.BlockSpec(memory_space=pltpu.VMEM)] * 3
        + [pl.BlockSpec(memory_space=pl.ANY)] * 3,
        out_specs=pl.BlockSpec(memory_space=pltpu.VMEM),
        scratch_shapes=[
            pltpu.VMEM((2, units, half), bf16),
            pltpu.VMEM((2, units, half), bf16),
            pltpu.VMEM((columns, units, COLS), bf16),
            pltpu.VMEM((EXPERTS, BLOCK, piece), bf16),
            pltpu.VMEM((2, n, BLOCK, piece), bf16),
            pltpu.VMEM((2, n * CAP, half), bf16),
            pltpu.VMEM((n * CAP, units), bf16),
            pltpu.VMEM((columns, n, BLOCK, lane), bf16),
            pltpu.VMEM((half // COLS, n, BLOCK, lane), bf16),
            pltpu.VMEM((half // COLS, n, BLOCK, lane), bf16),
            pltpu.SemaphoreType.DMA((2, parts)),
            pltpu.SemaphoreType.DMA((2, parts)),
            pltpu.SemaphoreType.DMA((columns,)),
            pltpu.SemaphoreType.DMA,
            pltpu.SemaphoreType.DMA,
            pltpu.SemaphoreType.DMA((2,)),
            pltpu.SemaphoreType.DMA((2, half // COLS)),
            pltpu.SemaphoreType.DMA((half // COLS,)),
            pltpu.SemaphoreType.DMA((half // COLS,)),
        ],
        compiler_params=pltpu.CompilerParams(
            collective_id=0, has_side_effects=True, vmem_limit_bytes=58 * 1024 * 1024
        ),
    )(tokens, expert_ids.T, gate_codes.T, gate_weight, up_weight, down_weight)


def solution(mesh):
    in_specs = (
        P(("groups", "expert"), "hidden"),
        P(("groups", "expert"), None),
        P(("groups", "expert"), None),
        P("expert", "hidden", None),
        P("expert", "hidden", None),
        P("expert", "hidden", None),
    )
    out_specs = P(("groups", "expert"), "hidden")
    return jax.shard_map(
        per_device, mesh=mesh, in_specs=in_specs, out_specs=out_specs, check_vma=False
    )
```

```python
import functools

import jax
import jax.numpy as jnp
from jax import lax
from jax.experimental import pallas as pl
from jax.experimental.pallas import tpu as pltpu
from jax.sharding import PartitionSpec as P

EXPERTS = 8
CAP = 4
GROUPS = 4
BLOCK = GROUPS * CAP
COLS = 1536
STEP = 896
MESH = pl.DeviceIdType.MESH


def hidden_steps(units):
    return [(at, min(STEP, units - at)) for at in range(0, units, STEP)]


def iota(shape, axis):
    return lax.broadcasted_iota(jnp.int32, shape, axis)


def moe_kernel(
    n, tok_ref, ids_ref, codes_ref, gate_hbm, up_hbm, down_hbm, out_ref,
    w_gate, w_up, w_down, send_rows, got_rows, rows, hidden, send_out, pair_out,
    got_out, gate_sem, up_sem, down_sem, rows_sent, rows_got, share_sem, pair_sem, out_sent,
    out_got,
):
    tok_dev, half = tok_ref.shape
    units, width = gate_hbm.shape[1:]
    steps = hidden_steps(units)
    per_half = half // COLS
    group = lax.axis_index("groups")
    me = lax.axis_index("expert")
    core = lax.axis_index("hidden")

    barrier = pltpu.get_barrier_semaphore()

    @pl.loop(1, n)
    def _(k):
        other = lax.rem(me + k, n)
        pl.semaphore_signal(barrier, inc=1, device_id=(group, other, core), device_id_type=MESH)

    pl.semaphore_signal(barrier, inc=1, device_id=(group, me, 1 - core), device_id_type=MESH)

    column = [pl.multiple_of(core * half, half), pl.multiple_of((1 - core) * half, half)]

    def fetch(source, target, sems, j, side):
        at, size = steps[j]
        return pltpu.make_async_copy(
            source.at[0, pl.ds(at, size), pl.ds(column[side], half)],
            target.at[side, pl.ds(at, size)],
            sems.at[side, j],
        )

    gate_copy = [[fetch(gate_hbm, w_gate, gate_sem, j, i) for i in range(2)] for j in range(len(steps))]
    up_copy = [[fetch(up_hbm, w_up, up_sem, j, i) for i in range(2)] for j in range(len(steps))]
    down_copy = [
        pltpu.make_async_copy(
            down_hbm.at[
                0, :, pl.ds(pl.multiple_of(column[1 - c // per_half] + c % per_half * COLS, COLS), COLS)
            ],
            w_down.at[c],
            down_sem.at[c],
        )
        for c in range(2 * per_half)
    ]
    def start_weights(some):
        for j in some:
            for side in range(2):
                gate_copy[j][side].start()
                up_copy[j][side].start()

    early = min(2, len(steps))
    start_weights(range(early))

    stacked = GROUPS * tok_dev
    slots = (stacked, EXPERTS * BLOCK)
    row, col = iota(slots, 0), iota(slots, 1)
    ids = jnp.concatenate([ids_ref[...].T] * GROUPS, axis=0)
    codes = jnp.concatenate([codes_ref[...].T] * GROUPS, axis=0)
    named = jnp.zeros(slots, jnp.bool_)
    code = jnp.zeros(slots, jnp.int32)
    for k in range(ids.shape[1]):
        same = ids[:, k:k + 1] == col // BLOCK
        named = named | same
        code = code + jnp.where(same, codes[:, k:k + 1], 0)
    square = (stacked, stacked)
    a, b = iota(square, 0), iota(square, 1)
    earlier = (a // tok_dev == b // tok_dev) & (b < a)
    place = jnp.dot(
        earlier.astype(jnp.float32).astype(jnp.bfloat16),
        named.astype(jnp.float32).astype(jnp.bfloat16),
        preferred_element_type=jnp.float32,
    ).astype(jnp.int32)
    hit = named & (place == col % CAP) & ((col // CAP) % GROUPS == row // tok_dev)
    pick = hit.astype(jnp.float32)
    high = pick * (code // 256).astype(jnp.float32) / 128.0
    low = pick * (code % 256).astype(jnp.float32) / 32768.0
    gains = jnp.concatenate([high, low], axis=0).astype(jnp.bfloat16)

    tok = tok_ref[...].astype(jnp.float32)
    piece = half // GROUPS
    tall = jnp.concatenate(
        [tok[:, g * piece:(g + 1) * piece] for g in range(GROUPS)], axis=0
    ).astype(jnp.bfloat16)
    send_rows[...] = (
        lax.dot_general(
            pick.T.astype(jnp.bfloat16), tall, (((1,), (0,)), ((), ())),
            preferred_element_type=jnp.float32,
        )
        .astype(jnp.bfloat16)
        .reshape(EXPERTS, BLOCK, piece)
    )

    pl.semaphore_wait(barrier, n)

    @pl.loop(1, n)
    def _(k):
        other = lax.rem(me + k, n)
        pltpu.make_async_remote_copy(
            src_ref=send_rows.at[lax.rem(other, EXPERTS)],
            dst_ref=got_rows.at[0, me],
            send_sem=rows_sent,
            recv_sem=rows_got,
            device_id=(group, other, core),
            device_id_type=MESH,
        ).start()

    pltpu.make_async_copy(
        send_rows.at[lax.rem(me, EXPERTS)], got_rows.at[0, me], rows_got
    ).start()

    start_weights(range(early, len(steps)))
    for copy in down_copy:
        copy.start()

    flat = EXPERTS * BLOCK
    lot = EXPERTS * CAP
    a, b = iota((flat, flat), 0), iota((flat, flat), 1)
    split = (a // lot) == (b // CAP) % GROUPS
    split = split & ((a % lot) // CAP == b // BLOCK) & (a % CAP == b % CAP)
    split = split.astype(jnp.float32).astype(jnp.bfloat16)
    join = (b // lot) == (a // CAP) % GROUPS
    join = join & ((b % lot) // CAP == a // BLOCK) & (b % CAP == a % CAP)
    join = join.astype(jnp.float32).astype(jnp.bfloat16)

    pltpu.make_async_copy(got_rows.at[0], got_rows.at[0], rows_got).wait()
    share = pltpu.make_async_remote_copy(
        src_ref=got_rows.at[0],
        dst_ref=got_rows.at[1],
        send_sem=share_sem.at[0],
        recv_sem=share_sem.at[1],
        device_id=(group, me, 1 - core),
        device_id_type=MESH,
    )
    share.start()

    def place_rows(side):
        for s in range(n // EXPERTS):
            block = got_rows[side, s * EXPERTS:(s + 1) * EXPERTS]
            block = jnp.dot(
                split, block.reshape(flat, piece), preferred_element_type=jnp.float32
            ).astype(jnp.bfloat16)
            for g in range(GROUPS):
                rows[side, s * lot:(s + 1) * lot, g * piece:(g + 1) * piece] = block[
                    g * lot:(g + 1) * lot
                ]

    def project(copies, weight, j, side):
        at, size = steps[j]
        copies[j][side].wait()
        return lax.dot_general(
            rows[side], weight[side, at:at + size], (((1,), (1,)), ((), ())),
            preferred_element_type=jnp.float32,
        )

    place_rows(0)
    for j, (at, size) in enumerate(steps):
        gate_pre = project(gate_copy, w_gate, j, 0)
        up_pre = project(up_copy, w_up, j, 0)
        if j == 0:
            share.wait()
            place_rows(1)
        gate_pre = gate_pre + project(gate_copy, w_gate, j, 1)
        up_pre = up_pre + project(up_copy, w_up, j, 1)
        silu = gate_pre / (1.0 + jnp.exp(-gate_pre))
        hidden[:, at:at + size] = (silu * up_pre).astype(jnp.bfloat16)

    lane = COLS // GROUPS
    pair = [
        pltpu.make_async_remote_copy(
            src_ref=send_out.at[c],
            dst_ref=pair_out.at[c],
            send_sem=pair_sem.at[0, c],
            recv_sem=pair_sem.at[1, c],
            device_id=(group, me, 1 - core),
            device_id_type=MESH,
        )
        for c in range(per_half)
    ]
    for c in range(2 * per_half):
        at = c % per_half
        down_copy[c].wait()
        out = jnp.dot(hidden[...], w_down[c], preferred_element_type=jnp.float32)
        out = out.astype(jnp.bfloat16)
        if c >= per_half:
            pair[at].wait_recv()
        for s in range(n // EXPERTS):
            span = slice(s * EXPERTS, (s + 1) * EXPERTS)
            block = jnp.concatenate(
                [
                    out[s * lot:(s + 1) * lot, g * lane:(g + 1) * lane]
                    for g in range(GROUPS)
                ],
                axis=0,
            )
            block = jnp.dot(join, block, preferred_element_type=jnp.float32)
            if c >= per_half:
                block = block + pair_out[at, span].reshape(flat, lane).astype(jnp.float32)
            send_out[c, span] = block.astype(jnp.bfloat16).reshape(EXPERTS, BLOCK, lane)
        if c < per_half:
            pair[c].start()
        else:

            @pl.loop(1, n)
            def _(k):
                other = lax.rem(me + k, n)
                pltpu.make_async_remote_copy(
                    src_ref=send_out.at[c, other],
                    dst_ref=got_out.at[at, me],
                    send_sem=out_sent.at[at],
                    recv_sem=out_got.at[at],
                    device_id=(group, other, core),
                    device_id_type=MESH,
                ).start()

            pltpu.make_async_copy(
                send_out.at[c, me], got_out.at[at, me], out_got.at[at]
            ).start()

    for at in range(per_half):
        landed = got_out.at[at]
        pltpu.make_async_copy(landed, landed, out_got.at[at]).wait()
        total = jnp.zeros((2 * stacked, lane), jnp.float32)
        for s in range(n // EXPERTS):
            block = got_out[at, s * EXPERTS:(s + 1) * EXPERTS].reshape(flat, lane)
            total = total + jnp.dot(gains, block, preferred_element_type=jnp.float32)
        mixed = total[:stacked] + total[stacked:]
        for g in range(GROUPS):
            to = at * COLS + g * lane
            out_ref[:, to:to + lane] = mixed[g * tok_dev:(g + 1) * tok_dev].astype(
                out_ref.dtype
            )

    for copy in pair:
        copy.wait_send()
    sent = got_rows.at[0, pl.ds(0, n - 1)]
    pltpu.make_async_copy(sent, sent, rows_sent).wait()
    for at in range(per_half):
        sent = got_out.at[at, pl.ds(0, n - 1)]
        pltpu.make_async_copy(sent, sent, out_sent.at[at]).wait()


def per_device(tokens, expert_ids, gate_codes, gate_weight, up_weight, down_weight):
    n = lax.axis_size("expert")
    tok_dev, half = tokens.shape
    units, width = gate_weight.shape[1:]
    parts = len(hidden_steps(units))
    columns = width // COLS
    lane = COLS // GROUPS
    piece = half // GROUPS
    bf16 = jnp.bfloat16
    return pl.pallas_call(
        functools.partial(moe_kernel, n),
        out_shape=jax.ShapeDtypeStruct((tok_dev, half), bf16),
        in_specs=[pl.BlockSpec(memory_space=pltpu.VMEM)] * 3
        + [pl.BlockSpec(memory_space=pl.ANY)] * 3,
        out_specs=pl.BlockSpec(memory_space=pltpu.VMEM),
        scratch_shapes=[
            pltpu.VMEM((2, units, half), bf16),
            pltpu.VMEM((2, units, half), bf16),
            pltpu.VMEM((columns, units, COLS), bf16),
            pltpu.VMEM((EXPERTS, BLOCK, piece), bf16),
            pltpu.VMEM((2, n, BLOCK, piece), bf16),
            pltpu.VMEM((2, n * CAP, half), bf16),
            pltpu.VMEM((n * CAP, units), bf16),
            pltpu.VMEM((columns, n, BLOCK, lane), bf16),
            pltpu.VMEM((half // COLS, n, BLOCK, lane), bf16),
            pltpu.VMEM((half // COLS, n, BLOCK, lane), bf16),
            pltpu.SemaphoreType.DMA((2, parts)),
            pltpu.SemaphoreType.DMA((2, parts)),
            pltpu.SemaphoreType.DMA((columns,)),
            pltpu.SemaphoreType.DMA,
            pltpu.SemaphoreType.DMA,
            pltpu.SemaphoreType.DMA((2,)),
            pltpu.SemaphoreType.DMA((2, half // COLS)),
            pltpu.SemaphoreType.DMA((half // COLS,)),
            pltpu.SemaphoreType.DMA((half // COLS,)),
        ],
        compiler_params=pltpu.CompilerParams(
            collective_id=0, has_side_effects=True, vmem_limit_bytes=58 * 1024 * 1024
        ),
    )(tokens, expert_ids.T, gate_codes.T, gate_weight, up_weight, down_weight)


def solution(mesh):
    in_specs = (
        P(("groups", "expert"), "hidden"),
        P(("groups", "expert"), None),
        P(("groups", "expert"), None),
        P("expert", "hidden", None),
        P("expert", "hidden", None),
        P("expert", "hidden", None),
    )
    out_specs = P(("groups", "expert"), "hidden")
    return jax.shard_map(
        per_device, mesh=mesh, in_specs=in_specs, out_specs=out_specs, check_vma=False
    )
```
